32 devices in a mesh: grp: 8 (over z, y), bfly: 4 (over x, core).
Axes of the slice: x: 2, y: 2, z: 4, core: 2. Of those that a mesh axis runs over, the one named last changes fastest.
Arguments:
- sources: bfloat16 [8, 4, 16, 256, 1024], P('grp', 'bfly'), may hold values from -6 to 6
- box_map: int32 [8, 4, 16], P('grp', 'bfly'), may hold values from 0 to 15, each once within a row
- compress: bfloat16 [8, 4, 16, 64, 256], P('grp', 'bfly'), may hold values from -0.375 to 0.375
- translate: bfloat16 [8, 4, 12, 16, 64, 128], P('grp', 'bfly'), may hold values from -0.5 to 0.5
- expand: bfloat16 [4, 16, 64, 256], P('bfly'), may hold values from -0.25 to 0.25
Outputs:
- field: bfloat16 [4, 16, 256, 1024], P('bfly', 'grp')
The draws below stay inside these ranges and needn't reach their ends.
All inputs are finite; a program needn't handle non-finite values.
Results may differ from the reference program's by a relative error of at most 0.03.
Values may be sent and summed in bfloat16 or wider, within the bound.
A program may use at most 128 MiB of HBM per device.

```python
import jax
import jax.numpy as jnp
from jax import lax

BOX = 256
R = 64
K = 16
LEVELS = 12
NV = 1024
N_GRP = 8
N_BFLY = 4


def levels(key, extent, shards, least, top_value):
    factor_of = 1.0
    for dim, parts in shards:
        steps = jax.random.uniform(jax.random.fold_in(jax.random.fold_in(key, 6), dim), (parts,), jnp.float32, least / len(shards), top_value / len(shards))
        factor_of = factor_of * jnp.repeat(jnp.exp(steps), extent[dim] // parts).reshape((-1,) + (1,) * (len(extent) - 1 - dim))
    return factor_of


def bell_draw(key, dims, spread, limit, cuts=(), kind=jnp.bfloat16):
    array = spread * jax.random.normal(key, dims, jnp.float32)
    if cuts:
        array = array * levels(key, dims, cuts, -0.22, 0.18)
    return jnp.clip(array, -limit, limit).astype(kind)


def setup_inputs(seed: int = 0) -> dict:
    key_of = jax.random.split(jax.random.key(seed), 6)
    return {
        "sources": bell_draw(key_of[0], (N_GRP, N_BFLY, K, BOX, NV), 1.0, 6.0, ((0, 8), (1, 4))),
        "box_map": jax.vmap(lambda own: jax.random.permutation(own, K))(jax.random.split(key_of[1], N_GRP * N_BFLY)).reshape((N_GRP, N_BFLY, K)).astype(jnp.int32),
        "compress": bell_draw(key_of[2], (N_GRP, N_BFLY, K, R, BOX), BOX ** -0.5, 0.375, ((0, 8), (1, 4))),
        "translate": bell_draw(key_of[3], (N_GRP, N_BFLY, LEVELS, K, R, 2 * R), (2 * R) ** -0.5, 0.5, ((0, 8), (1, 4))),
        "expand": bell_draw(key_of[4], (N_BFLY, K, R, BOX), (R * N_GRP) ** -0.5, 0.25, ((0, 4),)),
    }


def one_group(group_sources, group_map, group_compress, group_translate):
    bfly_size = N_BFLY
    bit_count = bfly_size.bit_length() - 1
    slot_bits = K.bit_length() - 1
    placed = jnp.take_along_axis(group_sources, group_map[:, :, None, None], axis=1)
    coeffs = jnp.einsum("djri,djiv->djrv", group_compress.astype(jnp.float32), placed.astype(jnp.float32)).astype(jnp.bfloat16)
    for section_no in range(LEVELS):
        if section_no < bit_count:
            far_state = coeffs[jnp.arange(bfly_size) ^ (1 << section_no)]
        else:
            far_state = coeffs[:, jnp.arange(K) ^ (1 << ((section_no - bit_count) % slot_bits))]
        own_part = jnp.einsum("djrs,djsv->djrv", group_translate[:, section_no, :, :, :R].astype(jnp.float32), coeffs.astype(jnp.float32))
        far_part = jnp.einsum("djrs,djsv->djrv", group_translate[:, section_no, :, :, R:].astype(jnp.float32), far_state.astype(jnp.float32))
        updated = own_part + far_part
        if section_no < LEVELS - 1:
            coeffs = updated.astype(jnp.bfloat16)
        else:
            coeffs = updated
    return coeffs


def reference(sources, box_map, compress, translate, expand):
    def add_group(summed, pieces):
        return summed + one_group(*pieces), None

    start_sum = jnp.zeros((N_BFLY, K, R, NV), jnp.float32)
    summed, unused = lax.scan(add_group, start_sum, (sources, box_map, compress, translate))
    field = jnp.einsum("djri,djrv->djiv", expand.astype(jnp.float32), summed, precision=lax.Precision.HIGHEST)
    return field.astype(jnp.bfloat16)
```

```python
import functools

import jax
import jax.numpy as jnp
from jax import lax
from jax.experimental import pallas as pl
from jax.experimental.pallas import tpu as pltpu
from jax.sharding import PartitionSpec as P

MESH = pl.DeviceIdType.MESH
F32 = jnp.float32
BF16 = jnp.bfloat16
CHUNKS = 4


def dot(a, b):
    return jnp.dot(a, b, preferred_element_type=F32)


def swap_halves(m):
    half = m.shape[1] // 2
    return jnp.concatenate([m[:, half:], m[:, :half]], axis=1)


class Plan:
    def __init__(self, n_grp, n_bfly, sources, compress, translate, expand):
        self.n_bfly = n_bfly
        self.bits = n_bfly.bit_length() - 1
        self.slots, self.rank, self.box = compress.shape[2:]
        self.levels = translate.shape[2]
        self.nv = sources.shape[-1]
        self.chunks = CHUNKS
        self.width = self.nv // self.chunks
        self.outer = min(4, n_grp)
        self.inner = n_grp // self.outer
        self.share = self.slots // n_grp
        self.pairs = (self.levels - self.bits) // 2
        assert self.slots == 16 and self.bits >= 1
        assert (self.levels - self.bits) % 2 == 0

    def strided(self, pair):
        return (2 * pair) % 4 == 2

    def member(self, pair, quad, place):
        return 4 * place + quad if self.strided(pair) else 4 * quad + place


def kernel(plan, map_ref, src_hbm, comp_hbm, trans_hbm, exp_hbm, out_hbm, *scratch):
    C, B, S, R = plan.chunks, plan.bits, plan.slots, plan.rank
    W, inner, outer, share = plan.width, plan.inner, plan.outer, plan.share
    scratch = list(scratch)
    src = [scratch.pop(0) for _ in range(C)]
    cats = [scratch.pop(0) for _ in range(B)]
    (comp, trans, expand, merged, wide, ping, pong, part, got_in, mid, got_out, done,
     src_sem, par_sem, out_sem, bsend, brecv, isend, irecv, osend, orecv) = scratch
    grp = lax.axis_index("grp")
    bfly = lax.axis_index("bfly")
    my_out, my_in = grp // inner, grp % inner

    def partner(level):
        bit = (bfly // (1 << level)) % 2
        return bfly + (1 << level) * (1 - 2 * bit)

    src_copies = [
        pltpu.make_async_copy(src_hbm.at[0, 0, :, :, pl.ds(c * W, W)], src[c], src_sem.at[c])
        for c in range(C)
    ]
    comp_copy = pltpu.make_async_copy(comp_hbm.at[0, 0], comp, par_sem.at[0])
    near_copy = pltpu.make_async_copy(trans_hbm.at[0, 0, pl.ds(0, B)], trans.at[pl.ds(0, B)], par_sem.at[1])
    rest_copy = pltpu.make_async_copy(
        trans_hbm.at[0, 0, pl.ds(B, plan.levels - B)], trans.at[pl.ds(B, plan.levels - B)], par_sem.at[2]
    )
    exp_copy = pltpu.make_async_copy(exp_hbm.at[0, pl.ds(grp * share, share)], expand, par_sem.at[3])
    comp_copy.start()
    src_copies[0].start()
    near_copy.start()
    for c in range(1, C):
        src_copies[c].start()
    rest_copy.start()
    exp_copy.start()

    peers = [(grp, partner(level)) for level in range(B)]
    in_peers = [(my_out * inner + (my_in + k) % inner, bfly) for k in range(1, inner)]
    out_peers = [(((my_out + k) % outer) * inner + my_in, bfly) for k in range(1, outer)]
    barrier = pltpu.get_barrier_semaphore()
    everyone = peers + in_peers + out_peers
    for peer in everyone:
        pl.semaphore_signal(barrier, inc=1, device_id=peer, device_id_type=MESH)
    pl.semaphore_wait(barrier, len(everyone))

    sends = []
    arrivals = {}

    def remote(key, source, target, send, recv, peer):
        copy = pltpu.make_async_remote_copy(
            src_ref=source, dst_ref=target, send_sem=send, recv_sem=recv,
            device_id=peer, device_id_type=MESH,
        )
        copy.start()
        sends.append(copy)
        arrivals[key] = copy

    def exchange(level, c):
        remote(
            ("b", level, c),
            cats[level].at[c, :, pl.ds(0, R)],
            cats[level].at[c, :, pl.ds(R, R)],
            bsend.at[level, c],
            brecv.at[level, c],
            peers[level],
        )

    def compress_stage(c):
        src_copies[c].wait()
        if c == 0:
            comp_copy.wait()
        for j in range(S):
            cats[0][c, j, 0:R, :] = dot(comp[j], src[c][map_ref[0, 0, j]]).astype(BF16)
        exchange(0, c)

    def far_stage(level, c):
        if c == 0 and level == 0:
            near_copy.wait()
        arrivals[("b", level, c)].wait_recv()
        for j in range(S):
            cats[level + 1][c, j, 0:R, :] = dot(trans[level, j], cats[level][c, j]).astype(BF16)
        exchange(level + 1, c)

    def merge_stage():
        rest_copy.wait()
        exp_copy.wait()
        for pair in range(plan.pairs):
            low = B + 2 * pair
            for quad in range(4):
                for place in range(4):
                    own = trans[low, plan.member(pair, quad, place)]
                    far = trans[low, plan.member(pair, quad, place ^ 2)]
                    if place & 1:
                        own, far = swap_halves(own), swap_halves(far)
                    zero = jnp.zeros_like(own)
                    if place & 2:
                        top, bottom = [zero, own], [far, zero]
                    else:
                        top, bottom = [own, zero], [zero, far]
                    block = jnp.concatenate(
                        [jnp.concatenate(top, axis=1), jnp.concatenate(bottom, axis=1)], axis=0
                    )
                    row = dot(trans[low + 1, plan.member(pair, quad, place)], block)
                    merged[pair, quad, place * R:(place + 1) * R, :] = row.astype(BF16)
        for s in range(share):
            wide[s] = expand[s].astype(F32).T.astype(BF16)

    def levels_stage(c):
        level = B - 1
        if level == 0 and c == 0:
            near_copy.wait()
        arrivals[("b", level, c)].wait_recv()
        for j in range(S):
            ping[j // 4, j % 4] = dot(trans[level, j], cats[level][c, j]).astype(BF16)
        now, later = ping, pong
        for pair in range(plan.pairs):
            for quad in range(4):
                picked = now[:, quad] if plan.strided(pair) else now[quad]
                value = dot(merged[pair, quad], picked.reshape(4 * R, W)).astype(BF16)
                value = value.reshape(4, R, W)
                if pair < plan.pairs - 1:
                    if plan.strided(pair):
                        later[:, quad] = value
                    else:
                        later[quad] = value
                else:
                    for place in range(4):
                        j = plan.member(pair, quad, place)
                        s, row = j // share, (j % share) * R
                        part[c, s % inner, s // inner, row:row + R, :] = value[place]
            now, later = later, now
        for k in range(1, inner):
            remote(
                ("i", k, c),
                part.at[c, (my_in + k) % inner],
                got_in.at[c, k - 1],
                isend.at[c, k - 1],
                irecv.at[c, k - 1],
                in_peers[k - 1],
            )

    def inner_stage(c):
        for k in range(1, inner):
            arrivals[("i", k, c)].wait_recv()
        total = part[c, my_in].astype(F32)
        for k in range(1, inner):
            total = total + got_in[c, k - 1].astype(F32)
        mid[c] = total.astype(BF16)
        for k in range(1, outer):
            remote(
                ("o", k, c),
                mid.at[c, (my_out + k) % outer],
                got_out.at[c, k - 1],
                osend.at[c, k - 1],
                orecv.at[c, k - 1],
                out_peers[k - 1],
            )

    out_copies = []

    def outer_stage(c):
        for k in range(1, outer):
            arrivals[("o", k, c)].wait_recv()
        total = mid[c, my_out].astype(F32)
        for k in range(1, outer):
            total = total + got_out[c, k - 1].astype(F32)
        upper = total.astype(BF16)
        lower = (total - upper.astype(F32)).astype(BF16)
        for s in range(share):
            rows = slice(s * R, (s + 1) * R)
            done[c, s] = (dot(wide[s], upper[rows]) + dot(wide[s], lower[rows])).astype(BF16)
        copy = pltpu.make_async_copy(done.at[c], out_hbm.at[0, :, :, pl.ds(c * W, W)], out_sem.at[c])
        copy.start()
        out_copies.append(copy)

    for t in range(C + B - 1):
        for level in reversed(range(B - 1)):
            if 0 <= t - 1 - level < C:
                far_stage(level, t - 1 - level)
        if t < C:
            compress_stage(t)
    merge_stage()
    for t in range(C + 2):
        if 0 <= t - 1 < C:
            inner_stage(t - 1)
        if 0 <= t - 2 < C:
            outer_stage(t - 2)
        if t < C:
            levels_stage(t)
    for copy in sends:
        copy.wait_send()
    for copy in out_copies:
        copy.wait()


def on_device(n_grp, n_bfly, sources, box_map, compress, translate, expand):
    plan = Plan(n_grp, n_bfly, sources, compress, translate, expand)
    C, B, S, R, W = plan.chunks, plan.bits, plan.slots, plan.rank, plan.width
    inner, outer, share = plan.inner, plan.outer, plan.share
    vm = pltpu.VMEM
    sem = pltpu.SemaphoreType.DMA
    any_space = pl.BlockSpec(memory_space=pl.ANY)
    return pl.pallas_call(
        functools.partial(kernel, plan),
        out_shape=jax.ShapeDtypeStruct((1, share, plan.box, plan.nv), BF16),
        in_specs=[pl.BlockSpec(memory_space=pltpu.SMEM)] + [any_space] * 4,
        out_specs=any_space,
        scratch_shapes=[vm((S, plan.box, W), BF16) for _ in range(C)]
        + [vm((C, S, 2 * R, W), BF16) for _ in range(B)]
        + [
            vm((S, R, plan.box), BF16),
            vm((plan.levels, S, R, 2 * R), BF16),
            vm((share, R, plan.box), BF16),
            vm((plan.pairs, 4, 4 * R, 4 * R), BF16),
            vm((share, plan.box, R), BF16),
            vm((4, 4, R, W), BF16),
            vm((4, 4, R, W), BF16),
            vm((C, inner, outer, share * R, W), BF16),
            vm((C, max(inner - 1, 1), outer, share * R, W), BF16),
            vm((C, outer, share * R, W), BF16),
            vm((C, max(outer - 1, 1), share * R, W), BF16),
            vm((C, share, plan.box, W), BF16),
            sem((C,)),
            sem((4,)),
            sem((C,)),
            sem((B, C)),
            sem((B, C)),
            sem((C, max(inner - 1, 1))),
            sem((C, max(inner - 1, 1))),
            sem((C, max(outer - 1, 1))),
            sem((C, max(outer - 1, 1))),
        ],
        compiler_params=pltpu.CompilerParams(
            collective_id=0, has_side_effects=True, vmem_limit_bytes=56 * 1024 * 1024
        ),
    )(box_map, sources, compress, translate, expand)


def solution(mesh):
    return jax.shard_map(
        functools.partial(on_device, mesh.shape["grp"], mesh.shape["bfly"]),
        mesh=mesh,
        in_specs=(
            P("grp", "bfly", None, None, None),
            P("grp", "bfly", None),
            P("grp", "bfly", None, None, None),
            P("grp", "bfly", None, None, None, None),
            P("bfly", None, None, None),
        ),
        out_specs=P("bfly", "grp", None, None),
        check_vma=False,
    )
```

```python
import functools

import jax
import jax.numpy as jnp
from jax import lax
from jax.experimental import pallas as pl
from jax.experimental.pallas import tpu as pltpu
from jax.sharding import PartitionSpec as P

MESH = pl.DeviceIdType.MESH
F32 = jnp.float32
BF16 = jnp.bfloat16
CHUNKS = 8


def dot(a, b):
    return jnp.dot(a, b, preferred_element_type=F32)


def swap_halves(m):
    half = m.shape[1] // 2
    return jnp.concatenate([m[:, half:], m[:, :half]], axis=1)


class Plan:
    def __init__(self, n_grp, n_bfly, sources, compress, translate, expand):
        self.n_bfly = n_bfly
        self.bits = n_bfly.bit_length() - 1
        self.slots, self.rank, self.box = compress.shape[2:]
        self.levels = translate.shape[2]
        self.nv = sources.shape[-1]
        self.chunks = CHUNKS
        self.width = self.nv // self.chunks
        self.outer = min(4, n_grp)
        self.inner = n_grp // self.outer
        self.share = self.slots // n_grp
        self.pairs = (self.levels - self.bits) // 2
        assert self.slots == 16 and self.bits >= 1
        assert (self.levels - self.bits) % 2 == 0

    def strided(self, pair):
        return (2 * pair) % 4 == 2

    def member(self, pair, quad, place):
        return 4 * place + quad if self.strided(pair) else 4 * quad + place


def kernel(plan, map_ref, src_hbm, comp_hbm, trans_hbm, exp_hbm, out_hbm, *scratch):
    C, B, S, R = plan.chunks, plan.bits, plan.slots, plan.rank
    W, inner, outer, share = plan.width, plan.inner, plan.outer, plan.share
    scratch = list(scratch)
    src = [scratch.pop(0) for _ in range(C)]
    cats = [scratch.pop(0) for _ in range(B)]
    (comp, trans, expand, merged, wide, ping, pong, part, got_in, mid, got_out, done,
     src_sem, par_sem, out_sem, bsend, brecv, isend, irecv, osend, orecv) = scratch
    grp = lax.axis_index("grp")
    bfly = lax.axis_index("bfly")
    my_out, my_in = grp // inner, grp % inner

    def partner(level):
        bit = (bfly // (1 << level)) % 2
        return bfly + (1 << level) * (1 - 2 * bit)

    src_copies = [
        pltpu.make_async_copy(src_hbm.at[0, 0, :, :, pl.ds(c * W, W)], src[c], src_sem.at[c])
        for c in range(C)
    ]
    comp_copy = pltpu.make_async_copy(comp_hbm.at[0, 0], comp, par_sem.at[0])
    near_copy = pltpu.make_async_copy(trans_hbm.at[0, 0, pl.ds(0, B)], trans.at[pl.ds(0, B)], par_sem.at[1])
    rest_copy = pltpu.make_async_copy(
        trans_hbm.at[0, 0, pl.ds(B, plan.levels - B)], trans.at[pl.ds(B, plan.levels - B)], par_sem.at[2]
    )
    exp_copy = pltpu.make_async_copy(exp_hbm.at[0, pl.ds(grp * share, share)], expand, par_sem.at[3])
    comp_copy.start()
    src_copies[0].start()
    near_copy.start()
    for c in range(1, C):
        src_copies[c].start()
    rest_copy.start()
    exp_copy.start()

    block_order = sorted(range(1, outer), key=lambda z: abs(2 * z - outer)) + [0]
    peers = [(grp, partner(level)) for level in range(B)]
    in_peers = [(my_out * inner + (my_in + k) % inner, bfly) for k in range(1, inner)]
    out_peers = [(((my_out + k) % outer) * inner + my_in, bfly) for k in range(1, outer)]
    barrier = pltpu.get_barrier_semaphore()
    everyone = peers + in_peers + out_peers
    for peer in everyone:
        pl.semaphore_signal(barrier, inc=1, device_id=peer, device_id_type=MESH)
    pl.semaphore_wait(barrier, len(everyone))

    sends = []
    arrivals = {}

    def remote(key, source, target, send, recv, peer):
        copy = pltpu.make_async_remote_copy(
            src_ref=source, dst_ref=target, send_sem=send, recv_sem=recv,
            device_id=peer, device_id_type=MESH,
        )
        copy.start()
        sends.append(copy)
        arrivals[key] = copy

    def exchange(level, c):
        remote(
            ("b", level, c),
            cats[level].at[c, :, pl.ds(0, R)],
            cats[level].at[c, :, pl.ds(R, R)],
            bsend.at[level, c],
            brecv.at[level, c],
            peers[level],
        )

    def compress_stage(c):
        src_copies[c].wait()
        if c == 0:
            comp_copy.wait()
        for j in range(S):
            cats[0][c, j, 0:R, :] = dot(comp[j], src[c][map_ref[0, 0, j]]).astype(BF16)
        exchange(0, c)

    def far_stage(level, c):
        if c == 0 and level == 0:
            near_copy.wait()
        arrivals[("b", level, c)].wait_recv()
        for j in range(S):
            cats[level + 1][c, j, 0:R, :] = dot(trans[level, j], cats[level][c, j]).astype(BF16)
        exchange(level + 1, c)

    def merge_stage():
        rest_copy.wait()
        exp_copy.wait()
        for pair in range(plan.pairs):
            low = B + 2 * pair
            for quad in range(4):
                for place in range(4):
                    own = trans[low, plan.member(pair, quad, place)]
                    far = trans[low, plan.member(pair, quad, place ^ 2)]
                    if place & 1:
                        own, far = swap_halves(own), swap_halves(far)
                    zero = jnp.zeros_like(own)
                    if place & 2:
                        top, bottom = [zero, own], [far, zero]
                    else:
                        top, bottom = [own, zero], [zero, far]
                    block = jnp.concatenate(
                        [jnp.concatenate(top, axis=1), jnp.concatenate(bottom, axis=1)], axis=0
                    )
                    row = dot(trans[low + 1, plan.member(pair, quad, place)], block)
                    merged[pair, quad, place * R:(place + 1) * R, :] = row.astype(BF16)
        for s in range(share):
            wide[s] = expand[s].astype(F32).T.astype(BF16)

    def levels_stage(c):
        level = B - 1
        if level == 0 and c == 0:
            near_copy.wait()
        arrivals[("b", level, c)].wait_recv()
        for j in range(S):
            ping[j // 4, j % 4] = dot(trans[level, j], cats[level][c, j]).astype(BF16)
        now, later = ping, pong
        for pair in range(plan.pairs):
            for quad in range(4):
                picked = now[:, quad] if plan.strided(pair) else now[quad]
                value = dot(merged[pair, quad], picked.reshape(4 * R, W)).astype(BF16)
                value = value.reshape(4, R, W)
                if pair < plan.pairs - 1:
                    if plan.strided(pair):
                        later[:, quad] = value
                    else:
                        later[quad] = value
                else:
                    for place in range(4):
                        j = plan.member(pair, quad, place)
                        s, row = j // share, (j % share) * R
                        part[c, s % inner, s // inner, row:row + R, :] = value[place]
            now, later = later, now
        for z in block_order:
            block = (my_out + z) % outer
            for k in range(1, inner):
                remote(
                    ("i", k, z, c),
                    part.at[c, (my_in + k) % inner, block],
                    got_in.at[c, k - 1, block],
                    isend.at[c, k - 1, z],
                    irecv.at[c, k - 1, z],
                    in_peers[k - 1],
                )

    def inner_stage(c):
        for z in block_order:
            block = (my_out + z) % outer
            for k in range(1, inner):
                arrivals[("i", k, z, c)].wait_recv()
            total = part[c, my_in, block].astype(F32)
            for k in range(1, inner):
                total = total + got_in[c, k - 1, block].astype(F32)
            mid[c, block] = total.astype(BF16)
            if z > 0:
                remote(
                    ("o", z, c),
                    mid.at[c, block],
                    got_out.at[c, z - 1],
                    osend.at[c, z - 1],
                    orecv.at[c, z - 1],
                    out_peers[z - 1],
                )

    out_copies = []

    def outer_stage(c):
        for k in range(1, outer):
            arrivals[("o", k, c)].wait_recv()
        total = mid[c, my_out].astype(F32)
        for k in range(1, outer):
            total = total + got_out[c, k - 1].astype(F32)
        upper = total.astype(BF16)
        lower = (total - upper.astype(F32)).astype(BF16)
        for s in range(share):
            rows = slice(s * R, (s + 1) * R)
            done[c, s] = (dot(wide[s], upper[rows]) + dot(wide[s], lower[rows])).astype(BF16)
        copy = pltpu.make_async_copy(done.at[c], out_hbm.at[0, :, :, pl.ds(c * W, W)], out_sem.at[c])
        copy.start()
        out_copies.append(copy)

    for t in range(C + B - 1):
        for level in reversed(range(B - 1)):
            if 0 <= t - 1 - level < C:
                far_stage(level, t - 1 - level)
        if t < C:
            compress_stage(t)
    merge_stage()
    for t in range(C + 2):
        if t < C:
            levels_stage(t)
        if 0 <= t - 1 < C:
            inner_stage(t - 1)
        if 0 <= t - 2 < C:
            outer_stage(t - 2)
    for copy in sends:
        copy.wait_send()
    for copy in out_copies:
        copy.wait()


def on_device(n_grp, n_bfly, sources, box_map, compress, translate, expand):
    plan = Plan(n_grp, n_bfly, sources, compress, translate, expand)
    C, B, S, R, W = plan.chunks, plan.bits, plan.slots, plan.rank, plan.width
    inner, outer, share = plan.inner, plan.outer, plan.share
    vm = pltpu.VMEM
    sem = pltpu.SemaphoreType.DMA
    any_space = pl.BlockSpec(memory_space=pl.ANY)
    return pl.pallas_call(
        functools.partial(kernel, plan),
        out_shape=jax.ShapeDtypeStruct((1, share, plan.box, plan.nv), BF16),
        in_specs=[pl.BlockSpec(memory_space=pltpu.SMEM)] + [any_space] * 4,
        out_specs=any_space,
        scratch_shapes=[vm((S, plan.box, W), BF16) for _ in range(C)]
        + [vm((C, S, 2 * R, W), BF16) for _ in range(B)]
        + [
            vm((S, R, plan.box), BF16),
            vm((plan.levels, S, R, 2 * R), BF16),
            vm((share, R, plan.box), BF16),
            vm((plan.pairs, 4, 4 * R, 4 * R), BF16),
            vm((share, plan.box, R), BF16),
            vm((4, 4, R, W), BF16),
            vm((4, 4, R, W), BF16),
            vm((C, inner, outer, share * R, W), BF16),
            vm((C, max(inner - 1, 1), outer, share * R, W), BF16),
            vm((C, outer, share * R, W), BF16),
            vm((C, max(outer - 1, 1), share * R, W), BF16),
            vm((C, share, plan.box, W), BF16),
            sem((C,)),
            sem((4,)),
            sem((C,)),
            sem((B, C)),
            sem((B, C)),
            sem((C, max(inner - 1, 1), outer)),
            sem((C, max(inner - 1, 1), outer)),
            sem((C, max(outer - 1, 1))),
            sem((C, max(outer - 1, 1))),
        ],
        compiler_params=pltpu.CompilerParams(
            collective_id=0, has_side_effects=True, vmem_limit_bytes=56 * 1024 * 1024
        ),
    )(box_map, sources, compress, translate, expand)


def solution(mesh):
    return jax.shard_map(
        functools.partial(on_device, mesh.shape["grp"], mesh.shape["bfly"]),
        mesh=mesh,
        in_specs=(
            P("grp", "bfly", None, None, None),
            P("grp", "bfly", None),
            P("grp", "bfly", None, None, None),
            P("grp", "bfly", None, None, None, None),
            P("bfly", None, None, None),
        ),
        out_specs=P("bfly", "grp", None, None),
        check_vma=False,
    )
```
